256 devices in a mesh: dom: 64 (over y, z, core), sub: 4 (over x).
Axes of the slice: x: 4, y: 4, z: 8, core: 2. Of those that a mesh axis runs over, the one named last changes fastest.
Arguments:
- features: bfloat16 [262144, 128], P(('dom', 'sub')), may hold values from -6 to 6
- weight: bfloat16 [128, 128], replicated, may hold values from -0.5 to 0.5
- layer_bias: float32 [128], replicated, may hold values from -3 to 3
- local_rows: int32 [24576], P(('dom', 'sub')), may hold values from 0 to 7, as said below
- local_blocks: int32 [24576], P(('dom', 'sub')), may hold values from 0 to 7, as said below
- local_values: bfloat16 [24576, 128, 128], P(('dom', 'sub')), may hold values from -0.09375 to 0.09375
- send_rows: int32 [65536, 12], P(('dom', 'sub')), may hold values from 0 to 1023
- bound_rows: int32 [24576], P(('dom', 'sub')), may hold values from 0 to 7, as said below
- bound_blocks: int32 [24576], P(('dom', 'sub')), may hold values from 0 to 23, as said below
- bound_values: bfloat16 [24576, 128, 128], P(('dom', 'sub')), may hold values from -0.09375 to 0.09375
- hub_rows: int32 [2048], P(('dom', 'sub')), may hold values from 0 to 1023
- hub_weights: bfloat16 [262144, 2048], P(('dom', 'sub')), may hold values from -0.078125 to 0.078125
Outputs:
- activated: bfloat16 [262144, 128], P(('dom', 'sub'))
The draws below stay inside these ranges and needn't reach their ends.
Inputs may be any that keep to these rules, and one draw needn't show every extreme that they name: `local_rows`: each device's 96 entries name every row tile of its nodes at least once. `local_blocks`: each device's entries name every block of 128 of its own nodes at least once; a pair of row tile and block may repeat. `bound_rows`: each device's 96 entries name every row tile of its nodes at least once. `bound_blocks`: each device's entries name every block of 128 received rows at least once; a pair may repeat.
All inputs are finite; a program needn't handle non-finite values.
Results may differ from the reference program's by a relative error of at most 0.0045.
Values may be sent and summed in bfloat16 or wider, within the bound.
No kernel may reach another device: no remote copies, remote signals or barrier semaphores. Data moves between devices by JAX's collectives and lax.ppermute only.
A program may use at most 128 MiB of HBM per device.

```python
import jax
import jax.numpy as jnp
from jax import lax

F = 128
H = 128
TILE = 128
ROWS_DEV = 1024
NTL = 96
NTB = 96
SLOT = 12
HUB_DEV = 8
SHARDS = 256
NODES = 262144
HUBS = 2048


def pair_table(key, tile_count, row_span, block_span):

    def one_device(device_key):
        key_rows, key_blocks, key_rperm, key_bperm, key_order = jax.random.split(device_key, 5)
        position = jnp.arange(tile_count, dtype=jnp.int32)
        rows_drawn = jax.random.randint(key_rows, (tile_count,), 0, row_span, dtype=jnp.int32)
        blocks_drawn = jax.random.randint(key_blocks, (tile_count,), 0, block_span, dtype=jnp.int32)
        row_perm = jax.random.permutation(key_rperm, row_span).astype(jnp.int32)
        block_perm = jax.random.permutation(key_bperm, block_span).astype(jnp.int32)
        rows_drawn = jnp.where(position < row_span, row_perm[position % row_span], rows_drawn)
        blocks_drawn = jnp.where(position < block_span, block_perm[position % block_span], blocks_drawn)
        shuffle = jax.random.permutation(key_order, tile_count)
        return (rows_drawn[shuffle], blocks_drawn[shuffle])
    device_keys = jax.random.split(key, SHARDS)
    rows_all, blocks_all = jax.vmap(one_device)(device_keys)
    return (rows_all.reshape(-1), blocks_all.reshape(-1))


def draw_local_rows(key, part):
    return pair_table(jax.random.fold_in(key, 1), NTL, ROWS_DEV // TILE, ROWS_DEV // TILE)[0]


def draw_local_blocks(key, part):
    return pair_table(jax.random.fold_in(key, 1), NTL, ROWS_DEV // TILE, ROWS_DEV // TILE)[1]


def draw_bound_rows(key, part):
    return pair_table(jax.random.fold_in(key, 2), NTB, ROWS_DEV // TILE, SHARDS * SLOT // TILE)[0]


def draw_bound_blocks(key, part):
    return pair_table(jax.random.fold_in(key, 2), NTB, ROWS_DEV // TILE, SHARDS * SLOT // TILE)[1]


def place_ends(array, key, least, high):
    dims = array.shape
    spot = [jax.random.randint(jax.random.fold_in(key, axis), (), 0, dims[axis]) for axis in range(len(dims))]
    array = array.at[tuple(spot)].set(least)
    longest = dims.index(max(dims))
    spot[longest] = (spot[longest] + 1) % dims[longest]
    return array.at[tuple(spot)].set(high)


def steps_of(key, extent, shards, smallest, largest):
    level, own = 1.0, jax.random.fold_in(key, 6)
    for dim, blocks in shards:
        steps = jnp.exp(jax.random.uniform(jax.random.fold_in(own, dim), (blocks,), jnp.float32, smallest / len(shards), largest / len(shards)))
        level = level * jnp.repeat(steps, extent[dim] // blocks).reshape([-1 if axis == dim else 1 for axis in range(len(extent))])
    return level


def gaussian(rng, dims, spread, bound, shards=(), held_as=jnp.bfloat16):
    gain = steps_of(rng, dims, shards, -0.22, 0.18) if shards else 1.0
    array = jax.random.normal(rng, dims, jnp.float32) * spread * gain
    return jnp.minimum(jnp.maximum(array, -bound), bound).astype(held_as)


def setup_inputs(seed: int = 0) -> dict:
    key_of = jax.random.split(jax.random.key(seed), 13)
    features = gaussian(key_of[0], (NODES, F), 1.0, 6.0, ((0, 256),))
    weight = gaussian(key_of[1], (F, H), F ** -0.5, 0.5)
    layer_bias = gaussian(key_of[2], (H,), 0.5, 3.0, (), jnp.float32)
    local_rows = draw_local_rows(jax.random.fold_in(key_of[12], 71), 0)
    local_blocks = draw_local_blocks(jax.random.fold_in(key_of[12], 71), 0)
    local_values = gaussian(key_of[5], (SHARDS * NTL, TILE, TILE), (3 * TILE * NTL // (ROWS_DEV // TILE)) ** -0.5, 0.09375, ((0, 256),))
    send_rows = place_ends(jax.random.randint(key_of[6], (SHARDS * SHARDS, SLOT), 0, ROWS_DEV), jax.random.fold_in(key_of[6], 1), 0, ROWS_DEV - 1).astype(jnp.int32)
    bound_rows = draw_bound_rows(jax.random.fold_in(key_of[12], 71), 0)
    bound_blocks = draw_bound_blocks(jax.random.fold_in(key_of[12], 71), 0)
    bound_values = gaussian(key_of[9], (SHARDS * NTB, TILE, TILE), (3 * TILE * NTB // (ROWS_DEV // TILE)) ** -0.5, 0.09375, ((0, 256),))
    hub_rows = place_ends(jax.random.randint(key_of[10], (HUBS,), 0, ROWS_DEV), jax.random.fold_in(key_of[10], 1), 0, ROWS_DEV - 1).astype(jnp.int32)
    hub_weights = gaussian(key_of[11], (NODES, HUBS), (3 * HUBS) ** -0.5, 0.078125, ((0, 256),))
    return {"features": features, "weight": weight, "layer_bias": layer_bias, "local_rows": local_rows, "local_blocks": local_blocks, "local_values": local_values, "send_rows": send_rows, "bound_rows": bound_rows, "bound_blocks": bound_blocks, "bound_values": bound_values, "hub_rows": hub_rows, "hub_weights": hub_weights}


def tile_total(rows_of, blocks_of, values, source):
    blocks = source.reshape(-1, TILE, H)[blocks_of]
    products = jnp.einsum("tij,tjh->tih", values.astype(jnp.float32), blocks.astype(jnp.float32))
    summed = jax.ops.segment_sum(products, rows_of, num_segments=ROWS_DEV // TILE)
    return summed.reshape(ROWS_DEV, H)


def reference(features, weight, layer_bias, local_rows, local_blocks, local_values, send_rows, bound_rows, bound_blocks, bound_values, hub_rows, hub_weights):
    mapped_all = jnp.dot(features, weight, preferred_element_type=jnp.float32).astype(jnp.bfloat16)
    mapped_dev = mapped_all.reshape(SHARDS, ROWS_DEV, H)
    owners = jnp.arange(SHARDS, dtype=jnp.int32)
    hub_ids = (owners[:, None] * ROWS_DEV + hub_rows.reshape(SHARDS, HUB_DEV)).reshape(-1)
    hub_mapped = mapped_all[hub_ids]
    sends = send_rows.reshape(SHARDS, SHARDS, SLOT).transpose(1, 0, 2)

    def per_device(inputs):
        device_id, own_rows, own_blocks, own_values, wanted, far_rows, far_blocks, far_values, hub_block = inputs
        own = mapped_dev[device_id]
        received = mapped_all[(owners[:, None] * ROWS_DEV + wanted).reshape(-1)]
        local_part = tile_total(own_rows, own_blocks, own_values, own)
        bound_part = tile_total(far_rows, far_blocks, far_values, received)
        hub_part = jnp.dot(hub_block, hub_mapped, preferred_element_type=jnp.float32)
        pre_act = local_part + bound_part + hub_part + layer_bias[None, :]
        return jax.nn.relu(pre_act).astype(jnp.bfloat16)

    result = lax.map(per_device, (
        owners,
        local_rows.reshape(SHARDS, NTL),
        local_blocks.reshape(SHARDS, NTL),
        local_values.reshape(SHARDS, NTL, TILE, TILE),
        sends,
        bound_rows.reshape(SHARDS, NTB),
        bound_blocks.reshape(SHARDS, NTB),
        bound_values.reshape(SHARDS, NTB, TILE, TILE),
        hub_weights.reshape(SHARDS, ROWS_DEV, HUBS),
    ))
    return result.reshape(NODES, H)
```

```python
import functools

import jax
import jax.numpy as jnp
from jax import lax
from jax.experimental import pallas as pl
from jax.experimental.pallas import tpu as pltpu
from jax.sharding import PartitionSpec as P

VMEM = pl.BlockSpec(memory_space=pltpu.VMEM)
SMEM = pl.BlockSpec(memory_space=pltpu.SMEM)
MIB = 1024 * 1024
Y, Z, CORES, X = 4, 8, 2, 4


def send_kernel(slot, send_ref, hub_ref, feat_ref, weight_ref, mapped_ref, out_ref, hub_out_ref, table, stage):
    mapped = jnp.dot(feat_ref[...], weight_ref[...], preferred_element_type=jnp.float32)
    mapped = mapped.astype(jnp.bfloat16)
    mapped_ref[...] = mapped
    table[...] = mapped.astype(jnp.float32)
    receivers = send_ref.shape[1]

    hub_rows = [table[pl.ds(hub_ref[j], 1), :] for j in range(hub_ref.shape[0])]
    hub_out_ref[...] = jnp.concatenate(hub_rows, axis=0).astype(jnp.bfloat16)

    group = 8

    def step(g, carry):
        base = pl.multiple_of(g * (group * slot), 8)
        for i in range(group):
            r = g * group + i
            for j in range(slot):
                stage[pl.ds(base + i * slot + j, 1), :] = table[pl.ds(send_ref[j, r], 1), :]
        rows = pl.ds(base, group * slot)
        out_ref[rows, :] = stage[rows, :].astype(jnp.bfloat16)
        return carry

    lax.fori_loop(0, receivers // group, step, 0)


def send_rows_of(features, weight, send_rows, hub_rows):
    rows, width = features.shape[0], weight.shape[1]
    receivers, slot = send_rows.shape
    return pl.pallas_call(
        functools.partial(send_kernel, slot),
        out_shape=(
            jax.ShapeDtypeStruct((rows, width), jnp.bfloat16),
            jax.ShapeDtypeStruct((receivers * slot, width), jnp.bfloat16),
            jax.ShapeDtypeStruct((hub_rows.shape[0], width), jnp.bfloat16),
        ),
        in_specs=[SMEM, SMEM, VMEM, VMEM],
        out_specs=(VMEM, VMEM, VMEM),
        scratch_shapes=[
            pltpu.VMEM((rows, width), jnp.float32),
            pltpu.VMEM((receivers * slot, width), jnp.float32),
        ],
        compiler_params=pltpu.CompilerParams(vmem_limit_bytes=16 * MIB),
        cost_estimate=pl.CostEstimate(flops=2 * rows * width * width, bytes_accessed=2 * MIB, transcendentals=0),
        name="send_rows",
    )(send_rows.T, hub_rows, features, weight)


def near_kernel(rows_ref, blocks_ref, values_ref, mapped_ref, bias_ref, out_ref):
    tile = values_ref.shape[1]
    out_ref[...] = jnp.broadcast_to(bias_ref[...], out_ref.shape)

    def step(t, carry):
        rows = pl.ds(pl.multiple_of(rows_ref[t] * tile, tile), tile)
        block = pl.ds(pl.multiple_of(blocks_ref[t] * tile, tile), tile)
        out_ref[rows, :] += jnp.dot(values_ref[t], mapped_ref[block, :], preferred_element_type=jnp.float32)
        return carry

    lax.fori_loop(0, values_ref.shape[0], step, 0, unroll=4)


def near_part(rows_of, blocks_of, values, mapped, bias):
    tiles, tile = values.shape[:2]
    rows, width = mapped.shape
    return pl.pallas_call(
        near_kernel,
        out_shape=jax.ShapeDtypeStruct((rows, width), jnp.float32),
        in_specs=[SMEM, SMEM, VMEM, VMEM, VMEM],
        out_specs=VMEM,
        compiler_params=pltpu.CompilerParams(vmem_limit_bytes=16 * MIB),
        cost_estimate=pl.CostEstimate(
            flops=2 * tiles * tile * tile * width, bytes_accessed=4 * MIB, transcendentals=0
        ),
        name="near_part",
    )(rows_of, blocks_of, values, mapped, bias)


def hub_kernel(near_ref, weights_ref, hub_ref, out_ref, ordered):
    own = hub_ref.shape[0] // (Y * Z * CORES * X)

    def place(i, carry):
        z = i % Z
        y = i // Z
        for core in range(CORES):
            for x in range(X):
                src = pl.multiple_of((((core * X + x) * Y + y) * Z + z) * own, own)
                dst = pl.multiple_of((((y * Z + z) * CORES + core) * X + x) * own, own)
                ordered[pl.ds(dst, own), :] = hub_ref[pl.ds(src, own), :].astype(jnp.float32)
        return carry

    lax.fori_loop(0, Y * Z, place, 0)
    hub = ordered[...].astype(jnp.bfloat16)
    tile = 256

    def step(i, carry):
        rows = pl.ds(pl.multiple_of(i * tile, tile), tile)
        out_ref[rows, :] = near_ref[rows, :] + jnp.dot(
            weights_ref[rows, :], hub, preferred_element_type=jnp.float32
        )
        return carry

    lax.fori_loop(0, out_ref.shape[0] // tile, step, 0)


def add_hub_part(near, weights, hub):
    rows, width = near.shape
    return pl.pallas_call(
        hub_kernel,
        out_shape=jax.ShapeDtypeStruct((rows, width), jnp.float32),
        in_specs=[VMEM, VMEM, VMEM],
        out_specs=VMEM,
        scratch_shapes=[pltpu.VMEM(hub.shape, jnp.float32)],
        compiler_params=pltpu.CompilerParams(vmem_limit_bytes=16 * MIB),
        cost_estimate=pl.CostEstimate(
            flops=2 * rows * hub.shape[0] * width, bytes_accessed=6 * MIB, transcendentals=0
        ),
        name="hub_part",
    )(near, weights, hub)


def far_kernel(rows_ref, blocks_ref, values_ref, received_ref, near_ref, out_ref, total):
    tile = values_ref.shape[1]
    total[...] = near_ref[...]

    def step(t, carry):
        rows = pl.ds(pl.multiple_of(rows_ref[t] * tile, tile), tile)
        block = pl.ds(pl.multiple_of(blocks_ref[t] * tile, tile), tile)
        total[rows, :] += jnp.dot(values_ref[t], received_ref[block, :], preferred_element_type=jnp.float32)
        return carry

    lax.fori_loop(0, values_ref.shape[0], step, 0, unroll=4)
    out_ref[...] = jnp.maximum(total[...], 0.0).astype(out_ref.dtype)


def finish(rows_of, blocks_of, values, received, near):
    tiles, tile = values.shape[:2]
    rows, width = near.shape
    return pl.pallas_call(
        far_kernel,
        out_shape=jax.ShapeDtypeStruct((rows, width), jnp.bfloat16),
        in_specs=[SMEM, SMEM, VMEM, VMEM, VMEM],
        out_specs=VMEM,
        scratch_shapes=[pltpu.VMEM((rows, width), jnp.float32)],
        compiler_params=pltpu.CompilerParams(vmem_limit_bytes=16 * MIB),
        cost_estimate=pl.CostEstimate(
            flops=2 * tiles * tile * tile * width, bytes_accessed=5 * MIB, transcendentals=0
        ),
        name="far_part",
    )(rows_of, blocks_of, values, received, near)


def partner(axis_size, stride, span, step):
    return [(i, i + ((((i // stride) % span) ^ step) - ((i // stride) % span)) * stride) for i in range(axis_size)]


def gather_hub(hub_here):
    dom = lax.axis_index("dom")
    sub = lax.axis_index("sub")
    dom_count, sub_count = lax.axis_size("dom"), lax.axis_size("sub")
    z, y, core = (dom // CORES) % Z, dom // (CORES * Z), dom % CORES
    rounds = [("dom", dom_count, CORES, Z, step, z) for step in (1, 2, 4)]
    rounds += [("dom", dom_count, CORES * Z, Y, step, y) for step in (1, 2)]
    rounds += [("sub", sub_count, 1, X, step, sub) for step in (1, 2)]
    rounds += [("dom", dom_count, 1, CORES, 1, core)]
    held = hub_here
    for axis, count, stride, span, step, place in rounds:
        other = lax.ppermute(held, axis, partner(count, stride, span, step))
        upper = (place // step) % 2 == 1
        held = jnp.concatenate(
            [jnp.where(upper, other, held), jnp.where(upper, held, other)], axis=0
        )
    return held


def on_device(
    features,
    weight,
    layer_bias,
    local_rows,
    local_blocks,
    local_values,
    send_rows,
    bound_rows,
    bound_blocks,
    bound_values,
    hub_rows,
    hub_weights,
):
    width = weight.shape[1]
    mapped, boundary_out, hub_here = send_rows_of(features, weight, send_rows, hub_rows)
    arrived = lax.all_to_all(
        boundary_out.reshape(-1, 2, width), ("dom", "sub"), split_axis=0, concat_axis=0, tiled=True
    )
    received = arrived.reshape(-1, width)
    near = near_part(local_rows, local_blocks, local_values, mapped, layer_bias[None, :])
    near = add_hub_part(near, hub_weights, gather_hub(hub_here))
    return finish(bound_rows, bound_blocks, bound_values, received, near)


def solution(mesh):
    in_specs = (
        P(("dom", "sub"), None),
        P(),
        P(),
        P(("dom", "sub")),
        P(("dom", "sub")),
        P(("dom", "sub"), None, None),
        P(("dom", "sub"), None),
        P(("dom", "sub")),
        P(("dom", "sub")),
        P(("dom", "sub"), None, None),
        P(("dom", "sub")),
        P(("dom", "sub"), None),
    )
    out_specs = P(("dom", "sub"), None)
    return jax.shard_map(
        on_device, mesh=mesh, in_specs=in_specs, out_specs=out_specs, check_vma=False
    )
```

```python
import functools

import jax
import jax.numpy as jnp
from jax import lax
from jax.experimental import pallas as pl
from jax.experimental.pallas import tpu as pltpu
from jax.sharding import PartitionSpec as P

VMEM = pl.BlockSpec(memory_space=pltpu.VMEM)
SMEM = pl.BlockSpec(memory_space=pltpu.SMEM)
MIB = 1024 * 1024
Y, Z, CORES, X = 4, 8, 2, 4


def send_kernel(
    core_ref, own_ref, other_ref, hub_ref, feat_ref, near_feat_ref, weight_ref, mapped_ref, out_ref, table, near_table, stage
):
    slot = own_ref.shape[0]
    hubs = hub_ref.shape[0]
    message = 2 * slot + hubs
    core = core_ref[0]
    mapped = jnp.dot(feat_ref[...], weight_ref[...], preferred_element_type=jnp.float32)
    mapped = mapped.astype(jnp.bfloat16)
    mapped_ref[...] = mapped
    table[...] = mapped.astype(jnp.float32)
    far = jnp.dot(near_feat_ref[...], weight_ref[...], preferred_element_type=jnp.float32)
    near_table[...] = far.astype(jnp.bfloat16).astype(jnp.float32)
    hub_rows = jnp.concatenate([table[pl.ds(hub_ref[j], 1), :] for j in range(hubs)], axis=0)

    def step(g, carry):
        base = pl.multiple_of(g * (X * message), X * message)
        for x in range(X):
            r = (g * CORES + core) * X + x
            for j in range(slot):
                stage[pl.ds(base + x * message + j, 1), :] = table[pl.ds(own_ref[j, r], 1), :]
            for j in range(slot):
                stage[pl.ds(base + x * message + slot + j, 1), :] = near_table[pl.ds(other_ref[j, r], 1), :]
            stage[pl.ds(base + x * message + 2 * slot, hubs), :] = hub_rows
        rows = pl.ds(base, X * message)
        out_ref[rows, :] = stage[rows, :].astype(jnp.bfloat16)
        return carry

    lax.fori_loop(0, Y * Z, step, 0)


def messages_of(core, send_own, send_other, hub_rows, features, near_features, weight):
    rows, width = features.shape[0], weight.shape[1]
    slot, hubs = send_own.shape[0], hub_rows.shape[0]
    total = Y * Z * X * (2 * slot + hubs)
    return pl.pallas_call(
        send_kernel,
        out_shape=(
            jax.ShapeDtypeStruct((rows, width), jnp.bfloat16),
            jax.ShapeDtypeStruct((total, width), jnp.bfloat16),
        ),
        in_specs=[SMEM, SMEM, SMEM, SMEM, VMEM, VMEM, VMEM],
        out_specs=(VMEM, VMEM),
        scratch_shapes=[
            pltpu.VMEM((rows, width), jnp.float32),
            pltpu.VMEM((rows, width), jnp.float32),
            pltpu.VMEM((total, width), jnp.float32),
        ],
        compiler_params=pltpu.CompilerParams(vmem_limit_bytes=16 * MIB),
        cost_estimate=pl.CostEstimate(flops=4 * rows * width * width, bytes_accessed=2 * MIB, transcendentals=0),
        name="messages",
    )(core, send_own, send_other, hub_rows, features, near_features, weight)


def near_kernel(rows_ref, blocks_ref, values_ref, mapped_ref, bias_ref, out_ref):
    tile = values_ref.shape[1]
    out_ref[...] = jnp.broadcast_to(bias_ref[...], out_ref.shape)

    def step(t, carry):
        rows = pl.ds(pl.multiple_of(rows_ref[t] * tile, tile), tile)
        block = pl.ds(pl.multiple_of(blocks_ref[t] * tile, tile), tile)
        out_ref[rows, :] += jnp.dot(values_ref[t], mapped_ref[block, :], preferred_element_type=jnp.float32)
        return carry

    lax.fori_loop(0, values_ref.shape[0], step, 0, unroll=4)


def near_part(rows_of, blocks_of, values, mapped, bias):
    tiles, tile = values.shape[:2]
    rows, width = mapped.shape
    return pl.pallas_call(
        near_kernel,
        out_shape=jax.ShapeDtypeStruct((rows, width), jnp.float32),
        in_specs=[SMEM, SMEM, VMEM, VMEM, VMEM],
        out_specs=VMEM,
        compiler_params=pltpu.CompilerParams(vmem_limit_bytes=16 * MIB),
        cost_estimate=pl.CostEstimate(
            flops=2 * tiles * tile * tile * width, bytes_accessed=4 * MIB, transcendentals=0
        ),
        name="near_part",
    )(rows_of, blocks_of, values, mapped, bias)


def order_kernel(slot, core_ref, arrived_ref, received_ref, hub_ref):
    message = arrived_ref.shape[0] // (Y * Z * X)
    hubs = message - 2 * slot
    size = X * message
    bound = CORES * X * slot
    core = core_ref[0]
    n = lax.broadcasted_iota(jnp.int32, (size, size), 0)
    source = lax.broadcasted_iota(jnp.int32, (size, size), 1)
    sender = (n >= X * slot).astype(jnp.int32)
    place = n - sender * (X * slot)
    x = sum((place >= k * slot).astype(jnp.int32) for k in range(1, X))
    second = jnp.where(sender == core, 0, slot)
    wanted = x * message + second + (place - x * slot)
    hub_place = n - bound
    hub_x = sum((hub_place >= k * hubs).astype(jnp.int32) for k in range(1, X))
    wanted = jnp.where(n >= bound, hub_x * message + 2 * slot + (hub_place - hub_x * hubs), wanted)
    order = jnp.where(wanted == source, 1.0, 0.0).astype(jnp.bfloat16)

    def step(g, carry):
        chunk = arrived_ref[pl.ds(pl.multiple_of(g * size, size), size), :]
        sorted_rows = jnp.dot(order, chunk, preferred_element_type=jnp.float32).astype(jnp.bfloat16)
        received_ref[pl.ds(pl.multiple_of(g * bound, bound), bound), :] = sorted_rows[:bound]
        hub_ref[pl.ds(pl.multiple_of(g * X * hubs, X * hubs), X * hubs), :] = sorted_rows[bound:]
        return carry

    lax.fori_loop(0, Y * Z, step, 0, unroll=4)


def order_rows(core, arrived, slot):
    total, width = arrived.shape
    groups = Y * Z
    bound = groups * CORES * X * slot
    hubs = total - bound
    return pl.pallas_call(
        functools.partial(order_kernel, slot),
        out_shape=(
            jax.ShapeDtypeStruct((bound, width), jnp.bfloat16),
            jax.ShapeDtypeStruct((hubs, width), jnp.bfloat16),
        ),
        in_specs=[SMEM, VMEM],
        out_specs=(VMEM, VMEM),
        compiler_params=pltpu.CompilerParams(vmem_limit_bytes=16 * MIB),
        cost_estimate=pl.CostEstimate(flops=256 * total * width, bytes_accessed=2 * MIB, transcendentals=0),
        name="order_rows",
    )(core, arrived)


def far_kernel(rows_ref, blocks_ref, values_ref, received_ref, near_ref, out_ref):
    tile = values_ref.shape[1]
    out_ref[...] = near_ref[...]

    def step(t, carry):
        rows = pl.ds(pl.multiple_of(rows_ref[t] * tile, tile), tile)
        block = pl.ds(pl.multiple_of(blocks_ref[t] * tile, tile), tile)
        out_ref[rows, :] += jnp.dot(values_ref[t], received_ref[block, :], preferred_element_type=jnp.float32)
        return carry

    lax.fori_loop(0, values_ref.shape[0], step, 0, unroll=4)


def add_far_part(rows_of, blocks_of, values, received, near):
    tiles, tile = values.shape[:2]
    rows, width = near.shape
    return pl.pallas_call(
        far_kernel,
        out_shape=jax.ShapeDtypeStruct((rows, width), jnp.float32),
        in_specs=[SMEM, SMEM, VMEM, VMEM, VMEM],
        out_specs=VMEM,
        compiler_params=pltpu.CompilerParams(vmem_limit_bytes=16 * MIB),
        cost_estimate=pl.CostEstimate(
            flops=2 * tiles * tile * tile * width, bytes_accessed=5 * MIB, transcendentals=0
        ),
        name="far_part",
    )(rows_of, blocks_of, values, received, near)


def hub_kernel(core_ref, sum_ref, weights_ref, own_ref, other_ref, out_ref, hub):
    groups = Y * Z
    half = own_ref.shape[0] // groups
    core = core_ref[0]

    def place(g, carry):
        rows = pl.ds(pl.multiple_of(g * half, half), half)
        own_at = pl.multiple_of((g * CORES + core) * half, half)
        other_at = pl.multiple_of((g * CORES + 1 - core) * half, half)
        hub[pl.ds(own_at, half), :] = own_ref[rows, :]
        hub[pl.ds(other_at, half), :] = other_ref[rows, :]
        return carry

    lax.fori_loop(0, groups, place, 0, unroll=4)
    tile = 256

    def step(i, carry):
        rows = pl.ds(pl.multiple_of(i * tile, tile), tile)
        total = sum_ref[rows, :] + jnp.dot(weights_ref[rows, :], hub[...], preferred_element_type=jnp.float32)
        out_ref[rows, :] = jnp.maximum(total, 0.0).astype(out_ref.dtype)
        return carry

    lax.fori_loop(0, out_ref.shape[0] // tile, step, 0)


def finish(core, total, weights, own_hub, other_hub):
    rows, width = total.shape
    hubs = weights.shape[1]
    return pl.pallas_call(
        hub_kernel,
        out_shape=jax.ShapeDtypeStruct((rows, width), jnp.bfloat16),
        in_specs=[SMEM, VMEM, VMEM, VMEM, VMEM],
        out_specs=VMEM,
        scratch_shapes=[pltpu.VMEM((hubs, width), jnp.bfloat16)],
        compiler_params=pltpu.CompilerParams(vmem_limit_bytes=16 * MIB),
        cost_estimate=pl.CostEstimate(flops=2 * rows * hubs * width, bytes_accessed=6 * MIB, transcendentals=0),
        name="hub_part",
    )(core, total, weights, own_hub, other_hub)


def on_device(
    features,
    weight,
    layer_bias,
    local_rows,
    local_blocks,
    local_values,
    send_rows,
    bound_rows,
    bound_blocks,
    bound_values,
    hub_rows,
    hub_weights,
):
    width = weight.shape[1]
    slot = send_rows.shape[1]
    dom_count, sub_count = lax.axis_size("dom"), lax.axis_size("sub")
    core = (lax.axis_index("dom") % CORES).astype(jnp.int32).reshape(1)
    other_core = [(i, i ^ 1) for i in range(dom_count)]
    same_core = [
        [i for i in range(dom_count * sub_count) if (i // sub_count) % CORES == c] for c in range(CORES)
    ]

    send_own = send_rows.T
    send_other = lax.ppermute(send_own, "dom", other_core)
    near_features = lax.ppermute(features, "dom", other_core)
    mapped, messages = messages_of(core, send_own, send_other, hub_rows, features, near_features, weight)
    arrived = lax.all_to_all(
        messages.reshape(len(same_core[0]), -1, width),
        ("dom", "sub"),
        split_axis=0,
        concat_axis=0,
        tiled=True,
        axis_index_groups=same_core,
    ).reshape(-1, width)
    near = near_part(local_rows, local_blocks, local_values, mapped, layer_bias[None, :])
    received, own_hub = order_rows(core, arrived, slot)
    other_hub = lax.ppermute(own_hub, "dom", other_core)
    total = add_far_part(bound_rows, bound_blocks, bound_values, received, near)
    return finish(core, total, hub_weights, own_hub, other_hub)


def solution(mesh):
    in_specs = (
        P(("dom", "sub"), None),
        P(),
        P(),
        P(("dom", "sub")),
        P(("dom", "sub")),
        P(("dom", "sub"), None, None),
        P(("dom", "sub"), None),
        P(("dom", "sub")),
        P(("dom", "sub")),
        P(("dom", "sub"), None, None),
        P(("dom", "sub")),
        P(("dom", "sub"), None),
    )
    out_specs = P(("dom", "sub"), None)
    return jax.shard_map(
        on_device, mesh=mesh, in_specs=in_specs, out_specs=out_specs, check_vma=False
    )
```

```python
import functools

import jax
import jax.numpy as jnp
from jax import lax
from jax.experimental import pallas as pl
from jax.experimental.pallas import tpu as pltpu
from jax.sharding import PartitionSpec as P

VMEM = pl.BlockSpec(memory_space=pltpu.VMEM)
SMEM = pl.BlockSpec(memory_space=pltpu.SMEM)
MIB = 1024 * 1024
Y, Z, CORES, X = 4, 8, 2, 4


def send_kernel(
    core_ref, own_hbm, other_hbm, hub_hbm, feat_hbm, near_feat_hbm, weight_hbm, mapped_ref, out_ref,
    own, other, hub, feat, near_feat, weight, table, near_table, stage, sems
):
    pairs = (
        (feat_hbm, feat), (weight_hbm, weight), (near_feat_hbm, near_feat),
        (own_hbm, own), (other_hbm, other), (hub_hbm, hub),
    )
    copies = [pltpu.make_async_copy(src, dst, sems.at[i]) for i, (src, dst) in enumerate(pairs)]
    for copy in copies:
        copy.start()
    slot = own.shape[0]
    hubs = hub.shape[0]
    message = 2 * slot + hubs
    core = core_ref[0]
    copies[0].wait()
    copies[1].wait()
    mapped = jnp.dot(feat[...], weight[...], preferred_element_type=jnp.float32)
    mapped = mapped.astype(jnp.bfloat16)
    mapped_ref[...] = mapped
    table[...] = mapped.astype(jnp.float32)
    copies[2].wait()
    far = jnp.dot(near_feat[...], weight[...], preferred_element_type=jnp.float32)
    near_table[...] = far.astype(jnp.bfloat16).astype(jnp.float32)
    for copy in copies[3:]:
        copy.wait()
    hub_rows = jnp.concatenate([table[pl.ds(hub[j], 1), :] for j in range(hubs)], axis=0)

    def step(g, carry):
        base = pl.multiple_of(g * (X * message), X * message)
        for x in range(X):
            r = (g * CORES + core) * X + x
            for j in range(slot):
                stage[pl.ds(base + x * message + j, 1), :] = table[pl.ds(own[j, r], 1), :]
            for j in range(slot):
                stage[pl.ds(base + x * message + slot + j, 1), :] = near_table[pl.ds(other[j, r], 1), :]
            stage[pl.ds(base + x * message + 2 * slot, hubs), :] = hub_rows
        rows = pl.ds(base, X * message)
        out_ref[rows, :] = stage[rows, :].astype(jnp.bfloat16)
        return carry

    lax.fori_loop(0, Y * Z, step, 0)


HBM = pl.BlockSpec(memory_space=pltpu.HBM)


def messages_of(core, send_own, send_other, hub_rows, features, near_features, weight):
    rows, width = features.shape[0], weight.shape[1]
    slot, hubs = send_own.shape[0], hub_rows.shape[0]
    total = Y * Z * X * (2 * slot + hubs)
    return pl.pallas_call(
        send_kernel,
        out_shape=(
            jax.ShapeDtypeStruct((rows, width), jnp.bfloat16),
            jax.ShapeDtypeStruct((total, width), jnp.bfloat16),
        ),
        in_specs=[SMEM, HBM, HBM, HBM, HBM, HBM, HBM],
        out_specs=(VMEM, VMEM),
        scratch_shapes=[
            pltpu.SMEM(send_own.shape, jnp.int32),
            pltpu.SMEM(send_own.shape, jnp.int32),
            pltpu.SMEM(hub_rows.shape, jnp.int32),
            pltpu.VMEM(features.shape, jnp.bfloat16),
            pltpu.VMEM(features.shape, jnp.bfloat16),
            pltpu.VMEM(weight.shape, jnp.bfloat16),
            pltpu.VMEM((rows, width), jnp.float32),
            pltpu.VMEM((rows, width), jnp.float32),
            pltpu.VMEM((total, width), jnp.float32),
            pltpu.SemaphoreType.DMA((6,)),
        ],
        compiler_params=pltpu.CompilerParams(vmem_limit_bytes=56 * MIB),
        cost_estimate=pl.CostEstimate(flops=4 * rows * width * width, bytes_accessed=2 * MIB, transcendentals=0),
        name="messages",
    )(core, send_own, send_other, hub_rows, features, near_features, weight)


def near_kernel(rows_ref, blocks_ref, values_ref, mapped_ref, bias_ref, out_ref):
    tile = values_ref.shape[1]
    out_ref[...] = jnp.broadcast_to(bias_ref[...], out_ref.shape)

    def step(t, carry):
        rows = pl.ds(pl.multiple_of(rows_ref[t] * tile, tile), tile)
        block = pl.ds(pl.multiple_of(blocks_ref[t] * tile, tile), tile)
        out_ref[rows, :] += jnp.dot(values_ref[t], mapped_ref[block, :], preferred_element_type=jnp.float32)
        return carry

    lax.fori_loop(0, values_ref.shape[0], step, 0, unroll=32)


def near_part(rows_of, blocks_of, values, mapped, bias):
    tiles, tile = values.shape[:2]
    rows, width = mapped.shape
    return pl.pallas_call(
        near_kernel,
        out_shape=jax.ShapeDtypeStruct((rows, width), jnp.float32),
        in_specs=[SMEM, SMEM, VMEM, VMEM, VMEM],
        out_specs=VMEM,
        compiler_params=pltpu.CompilerParams(vmem_limit_bytes=16 * MIB),
        cost_estimate=pl.CostEstimate(
            flops=2 * tiles * tile * tile * width, bytes_accessed=4 * MIB, transcendentals=0
        ),
        name="near_part",
    )(rows_of, blocks_of, values, mapped, bias)


def order_kernel(slot, core_ref, arrived_ref, after_ref, received_ref, hub_ref):
    message = arrived_ref.shape[0] // (Y * Z * X)
    hubs = message - 2 * slot
    size = X * message
    bound = CORES * X * slot
    core = core_ref[0]
    n = lax.broadcasted_iota(jnp.int32, (size, size), 0)
    source = lax.broadcasted_iota(jnp.int32, (size, size), 1)
    sender = (n >= X * slot).astype(jnp.int32)
    place = n - sender * (X * slot)
    x = sum((place >= k * slot).astype(jnp.int32) for k in range(1, X))
    second = jnp.where(sender == core, 0, slot)
    wanted = x * message + second + (place - x * slot)
    hub_place = n - bound
    hub_x = sum((hub_place >= k * hubs).astype(jnp.int32) for k in range(1, X))
    wanted = jnp.where(n >= bound, hub_x * message + 2 * slot + (hub_place - hub_x * hubs), wanted)
    order = jnp.where(wanted == source, 1.0, 0.0).astype(jnp.bfloat16)

    def step(g, carry):
        chunk = arrived_ref[pl.ds(pl.multiple_of(g * size, size), size), :]
        sorted_rows = jnp.dot(order, chunk, preferred_element_type=jnp.float32).astype(jnp.bfloat16)
        received_ref[pl.ds(pl.multiple_of(g * bound, bound), bound), :] = sorted_rows[:bound]
        hub_ref[pl.ds(pl.multiple_of(g * X * hubs, X * hubs), X * hubs), :] = sorted_rows[bound:]
        return carry

    lax.fori_loop(0, Y * Z, step, 0, unroll=16)


def order_rows(core, arrived, slot, after):
    total, width = arrived.shape
    groups = Y * Z
    bound = groups * CORES * X * slot
    hubs = total - bound
    return pl.pallas_call(
        functools.partial(order_kernel, slot),
        out_shape=(
            jax.ShapeDtypeStruct((bound, width), jnp.bfloat16),
            jax.ShapeDtypeStruct((hubs, width), jnp.bfloat16),
        ),
        in_specs=[SMEM, VMEM, pl.BlockSpec(memory_space=pl.ANY)],
        out_specs=(VMEM, VMEM),
        compiler_params=pltpu.CompilerParams(vmem_limit_bytes=16 * MIB),
        cost_estimate=pl.CostEstimate(flops=256 * total * width, bytes_accessed=2 * MIB, transcendentals=0),
        name="order_rows",
    )(core, arrived, after)


def far_kernel(rows_ref, blocks_ref, values_ref, received_ref, near_ref, out_ref):
    tile = values_ref.shape[1]
    out_ref[...] = near_ref[...]

    def step(t, carry):
        rows = pl.ds(pl.multiple_of(rows_ref[t] * tile, tile), tile)
        block = pl.ds(pl.multiple_of(blocks_ref[t] * tile, tile), tile)
        out_ref[rows, :] += jnp.dot(values_ref[t], received_ref[block, :], preferred_element_type=jnp.float32)
        return carry

    lax.fori_loop(0, values_ref.shape[0], step, 0, unroll=32)


def add_far_part(rows_of, blocks_of, values, received, near):
    tiles, tile = values.shape[:2]
    rows, width = near.shape
    return pl.pallas_call(
        far_kernel,
        out_shape=jax.ShapeDtypeStruct((rows, width), jnp.float32),
        in_specs=[SMEM, SMEM, VMEM, VMEM, VMEM],
        out_specs=VMEM,
        compiler_params=pltpu.CompilerParams(vmem_limit_bytes=16 * MIB),
        cost_estimate=pl.CostEstimate(
            flops=2 * tiles * tile * tile * width, bytes_accessed=5 * MIB, transcendentals=0
        ),
        name="far_part",
    )(rows_of, blocks_of, values, received, near)


def hub_kernel(core_ref, sum_ref, weights_ref, own_ref, other_ref, out_ref, hub):
    groups = Y * Z
    half = own_ref.shape[0] // groups
    core = core_ref[0]

    def place(g, carry):
        rows = pl.ds(pl.multiple_of(g * half, half), half)
        own_at = pl.multiple_of((g * CORES + core) * half, half)
        other_at = pl.multiple_of((g * CORES + 1 - core) * half, half)
        hub[pl.ds(own_at, half), :] = own_ref[rows, :]
        hub[pl.ds(other_at, half), :] = other_ref[rows, :]
        return carry

    lax.fori_loop(0, groups, place, 0, unroll=8)
    tile = 256

    def step(i, carry):
        rows = pl.ds(pl.multiple_of(i * tile, tile), tile)
        total = sum_ref[rows, :] + jnp.dot(weights_ref[rows, :], hub[...], preferred_element_type=jnp.float32)
        out_ref[rows, :] = jnp.maximum(total, 0.0).astype(out_ref.dtype)
        return carry

    lax.fori_loop(0, out_ref.shape[0] // tile, step, 0)


def finish(core, total, weights, own_hub, other_hub):
    rows, width = total.shape
    hubs = weights.shape[1]
    return pl.pallas_call(
        hub_kernel,
        out_shape=jax.ShapeDtypeStruct((rows, width), jnp.bfloat16),
        in_specs=[SMEM, VMEM, VMEM, VMEM, VMEM],
        out_specs=VMEM,
        scratch_shapes=[pltpu.VMEM((hubs, width), jnp.bfloat16)],
        compiler_params=pltpu.CompilerParams(vmem_limit_bytes=16 * MIB),
        cost_estimate=pl.CostEstimate(flops=2 * rows * hubs * width, bytes_accessed=6 * MIB, transcendentals=0),
        name="hub_part",
    )(core, total, weights, own_hub, other_hub)


def on_device(
    features,
    weight,
    layer_bias,
    local_rows,
    local_blocks,
    local_values,
    send_rows,
    bound_rows,
    bound_blocks,
    bound_values,
    hub_rows,
    hub_weights,
):
    width = weight.shape[1]
    slot = send_rows.shape[1]
    dom_count, sub_count = lax.axis_size("dom"), lax.axis_size("sub")
    core = (lax.axis_index("dom") % CORES).astype(jnp.int32).reshape(1)
    other_core = [(i, i ^ 1) for i in range(dom_count)]
    same_core = [
        [i for i in range(dom_count * sub_count) if (i // sub_count) % CORES == c] for c in range(CORES)
    ]

    send_own = send_rows.T
    send_other = lax.ppermute(send_own, "dom", other_core)
    near_features = lax.ppermute(features, "dom", other_core)
    mapped, messages = messages_of(core, send_own, send_other, hub_rows, features, near_features, weight)
    arrived = lax.all_to_all(
        messages.reshape(len(same_core[0]), -1, width),
        ("dom", "sub"),
        split_axis=0,
        concat_axis=0,
        tiled=True,
        axis_index_groups=same_core,
    ).reshape(-1, width)
    near = near_part(local_rows, local_blocks, local_values, mapped, layer_bias[None, :])
    received, own_hub = order_rows(core, arrived, slot, near)
    other_hub = lax.ppermute(own_hub, "dom", other_core)
    total = add_far_part(bound_rows, bound_blocks, bound_values, received, near)
    return finish(core, total, hub_weights, own_hub, other_hub)


def solution(mesh):
    in_specs = (
        P(("dom", "sub"), None),
        P(),
        P(),
        P(("dom", "sub")),
        P(("dom", "sub")),
        P(("dom", "sub"), None, None),
        P(("dom", "sub"), None),
        P(("dom", "sub")),
        P(("dom", "sub")),
        P(("dom", "sub"), None, None),
        P(("dom", "sub")),
        P(("dom", "sub"), None),
    )
    out_specs = P(("dom", "sub"), None)
    return jax.shard_map(
        on_device, mesh=mesh, in_specs=in_specs, out_specs=out_specs, check_vma=False
    )
```

```python
import functools

import jax
import jax.numpy as jnp
from jax import lax
from jax.experimental import pallas as pl
from jax.experimental.pallas import tpu as pltpu
from jax.sharding import PartitionSpec as P

VMEM = pl.BlockSpec(memory_space=pltpu.VMEM)
SMEM = pl.BlockSpec(memory_space=pltpu.SMEM)
MIB = 1024 * 1024
Y, Z, CORES, X = 4, 8, 2, 4


def send_kernel(
    core_ref, own_hbm, other_hbm, hub_hbm, feat_hbm, near_feat_hbm, weight_hbm, mapped_ref, out_ref,
    own, other, hub, feat, near_feat, weight, table, near_table, stage, sems
):
    pairs = (
        (feat_hbm, feat), (weight_hbm, weight), (near_feat_hbm, near_feat),
        (own_hbm, own), (other_hbm, other), (hub_hbm, hub),
    )
    copies = [pltpu.make_async_copy(src, dst, sems.at[i]) for i, (src, dst) in enumerate(pairs)]
    for copy in copies:
        copy.start()
    slot = own.shape[0]
    hubs = hub.shape[0]
    message = 2 * slot + hubs
    core = core_ref[0]
    copies[0].wait()
    copies[1].wait()
    mapped = jnp.dot(feat[...], weight[...], preferred_element_type=jnp.float32)
    mapped = mapped.astype(jnp.bfloat16)
    mapped_ref[...] = mapped
    table[...] = mapped.astype(jnp.float32)
    copies[2].wait()
    far = jnp.dot(near_feat[...], weight[...], preferred_element_type=jnp.float32)
    near_table[...] = far.astype(jnp.bfloat16).astype(jnp.float32)
    for copy in copies[3:]:
        copy.wait()
    hub_rows = jnp.concatenate([table[pl.ds(hub[j], 1), :] for j in range(hubs)], axis=0)

    def step(g, carry):
        base = pl.multiple_of(g * (X * message), X * message)
        for x in range(X):
            r = (g * CORES + core) * X + x
            for j in range(slot):
                stage[pl.ds(base + x * message + j, 1), :] = table[pl.ds(own[j, r], 1), :]
            for j in range(slot):
                stage[pl.ds(base + x * message + slot + j, 1), :] = near_table[pl.ds(other[j, r], 1), :]
            stage[pl.ds(base + x * message + 2 * slot, hubs), :] = hub_rows
        rows = pl.ds(base, X * message)
        out_ref[rows, :] = stage[rows, :].astype(jnp.bfloat16)
        return carry

    lax.fori_loop(0, Y * Z, step, 0)


HBM = pl.BlockSpec(memory_space=pltpu.HBM)


def messages_of(core, send_own, send_other, hub_rows, features, near_features, weight):
    rows, width = features.shape[0], weight.shape[1]
    slot, hubs = send_own.shape[0], hub_rows.shape[0]
    total = Y * Z * X * (2 * slot + hubs)
    return pl.pallas_call(
        send_kernel,
        out_shape=(
            jax.ShapeDtypeStruct((rows, width), jnp.bfloat16),
            jax.ShapeDtypeStruct((total, width), jnp.bfloat16),
        ),
        in_specs=[SMEM, HBM, HBM, HBM, HBM, HBM, HBM],
        out_specs=(VMEM, VMEM),
        scratch_shapes=[
            pltpu.SMEM(send_own.shape, jnp.int32),
            pltpu.SMEM(send_own.shape, jnp.int32),
            pltpu.SMEM(hub_rows.shape, jnp.int32),
            pltpu.VMEM(features.shape, jnp.bfloat16),
            pltpu.VMEM(features.shape, jnp.bfloat16),
            pltpu.VMEM(weight.shape, jnp.bfloat16),
            pltpu.VMEM((rows, width), jnp.float32),
            pltpu.VMEM((rows, width), jnp.float32),
            pltpu.VMEM((total, width), jnp.float32),
            pltpu.SemaphoreType.DMA((6,)),
        ],
        compiler_params=pltpu.CompilerParams(vmem_limit_bytes=56 * MIB),
        cost_estimate=pl.CostEstimate(flops=4 * rows * width * width, bytes_accessed=2 * MIB, transcendentals=0),
        name="messages",
    )(core, send_own, send_other, hub_rows, features, near_features, weight)


def near_kernel(rows_ref, blocks_ref, values_ref, mapped_ref, bias_ref, out_ref):
    tile = values_ref.shape[1]
    out_ref[...] = jnp.broadcast_to(bias_ref[...], out_ref.shape)

    def step(t, carry):
        rows = pl.ds(pl.multiple_of(rows_ref[t] * tile, tile), tile)
        block = pl.ds(pl.multiple_of(blocks_ref[t] * tile, tile), tile)
        out_ref[rows, :] += jnp.dot(values_ref[t], mapped_ref[block, :], preferred_element_type=jnp.float32)
        return carry

    lax.fori_loop(0, values_ref.shape[0], step, 0, unroll=32)


def near_part(rows_of, blocks_of, values, mapped, bias):
    tiles, tile = values.shape[:2]
    rows, width = mapped.shape
    return pl.pallas_call(
        near_kernel,
        out_shape=jax.ShapeDtypeStruct((rows, width), jnp.float32),
        in_specs=[SMEM, SMEM, VMEM, VMEM, VMEM],
        out_specs=VMEM,
        compiler_params=pltpu.CompilerParams(vmem_limit_bytes=16 * MIB),
        cost_estimate=pl.CostEstimate(
            flops=2 * tiles * tile * tile * width, bytes_accessed=4 * MIB, transcendentals=0
        ),
        name="near_part",
    )(rows_of, blocks_of, values, mapped, bias)


def order_kernel(slot, core_ref, arrived_ref, after_ref, received_ref, hub_ref):
    message = arrived_ref.shape[0] // (Y * Z * X)
    hubs = message - 2 * slot
    size = X * message
    bound = CORES * X * slot
    core = core_ref[0]
    n = lax.broadcasted_iota(jnp.int32, (size, size), 0)
    source = lax.broadcasted_iota(jnp.int32, (size, size), 1)
    sender = (n >= X * slot).astype(jnp.int32)
    place = n - sender * (X * slot)
    x = sum((place >= k * slot).astype(jnp.int32) for k in range(1, X))
    second = jnp.where(sender == core, 0, slot)
    wanted = x * message + second + (place - x * slot)
    hub_place = n - bound
    hub_x = sum((hub_place >= k * hubs).astype(jnp.int32) for k in range(1, X))
    wanted = jnp.where(n >= bound, hub_x * message + 2 * slot + (hub_place - hub_x * hubs), wanted)
    order = jnp.where(wanted == source, 1.0, 0.0).astype(jnp.bfloat16)

    def step(g, carry):
        chunk = arrived_ref[pl.ds(pl.multiple_of(g * size, size), size), :]
        sorted_rows = jnp.dot(order, chunk, preferred_element_type=jnp.float32).astype(jnp.bfloat16)
        received_ref[pl.ds(pl.multiple_of(g * bound, bound), bound), :] = sorted_rows[:bound]
        hub_ref[pl.ds(pl.multiple_of(g * X * hubs, X * hubs), X * hubs), :] = sorted_rows[bound:]
        return carry

    lax.fori_loop(0, Y * Z, step, 0, unroll=16)


def order_rows(core, arrived, slot, after):
    total, width = arrived.shape
    groups = Y * Z
    bound = groups * CORES * X * slot
    hubs = total - bound
    return pl.pallas_call(
        functools.partial(order_kernel, slot),
        out_shape=(
            jax.ShapeDtypeStruct((bound, width), jnp.bfloat16),
            jax.ShapeDtypeStruct((hubs, width), jnp.bfloat16),
        ),
        in_specs=[SMEM, VMEM, pl.BlockSpec(memory_space=pl.ANY)],
        out_specs=(VMEM, VMEM),
        compiler_params=pltpu.CompilerParams(vmem_limit_bytes=16 * MIB),
        cost_estimate=pl.CostEstimate(flops=8000000000, bytes_accessed=16 * MIB, transcendentals=0),
        name="order_rows",
    )(core, arrived, after)


def far_kernel(rows_ref, blocks_ref, values_ref, received_ref, near_ref, out_ref):
    tile = values_ref.shape[1]
    out_ref[...] = near_ref[...]

    def step(t, carry):
        rows = pl.ds(pl.multiple_of(rows_ref[t] * tile, tile), tile)
        block = pl.ds(pl.multiple_of(blocks_ref[t] * tile, tile), tile)
        out_ref[rows, :] += jnp.dot(values_ref[t], received_ref[block, :], preferred_element_type=jnp.float32)
        return carry

    lax.fori_loop(0, values_ref.shape[0], step, 0, unroll=32)


def add_far_part(rows_of, blocks_of, values, received, near):
    tiles, tile = values.shape[:2]
    rows, width = near.shape
    return pl.pallas_call(
        far_kernel,
        out_shape=jax.ShapeDtypeStruct((rows, width), jnp.float32),
        in_specs=[SMEM, SMEM, VMEM, VMEM, VMEM],
        out_specs=VMEM,
        compiler_params=pltpu.CompilerParams(vmem_limit_bytes=16 * MIB),
        cost_estimate=pl.CostEstimate(
            flops=2 * tiles * tile * tile * width, bytes_accessed=5 * MIB, transcendentals=0
        ),
        name="far_part",
    )(rows_of, blocks_of, values, received, near)


def hub_kernel(core_ref, sum_ref, weights_ref, own_ref, other_ref, out_ref, hub):
    groups = Y * Z
    half = own_ref.shape[0] // groups
    core = core_ref[0]

    def place(g, carry):
        rows = pl.ds(pl.multiple_of(g * half, half), half)
        own_at = pl.multiple_of((g * CORES + core) * half, half)
        other_at = pl.multiple_of((g * CORES + 1 - core) * half, half)
        hub[pl.ds(own_at, half), :] = own_ref[rows, :]
        hub[pl.ds(other_at, half), :] = other_ref[rows, :]
        return carry

    lax.fori_loop(0, groups, place, 0, unroll=8)
    tile = 256

    def step(i, carry):
        rows = pl.ds(pl.multiple_of(i * tile, tile), tile)
        total = sum_ref[rows, :] + jnp.dot(weights_ref[rows, :], hub[...], preferred_element_type=jnp.float32)
        out_ref[rows, :] = jnp.maximum(total, 0.0).astype(out_ref.dtype)
        return carry

    lax.fori_loop(0, out_ref.shape[0] // tile, step, 0)


def finish(core, total, weights, own_hub, other_hub):
    rows, width = total.shape
    hubs = weights.shape[1]
    return pl.pallas_call(
        hub_kernel,
        out_shape=jax.ShapeDtypeStruct((rows, width), jnp.bfloat16),
        in_specs=[SMEM, VMEM, VMEM, VMEM, VMEM],
        out_specs=VMEM,
        scratch_shapes=[pltpu.VMEM((hubs, width), jnp.bfloat16)],
        compiler_params=pltpu.CompilerParams(vmem_limit_bytes=16 * MIB),
        cost_estimate=pl.CostEstimate(flops=2 * rows * hubs * width, bytes_accessed=6 * MIB, transcendentals=0),
        name="hub_part",
    )(core, total, weights, own_hub, other_hub)


def on_device(
    features,
    weight,
    layer_bias,
    local_rows,
    local_blocks,
    local_values,
    send_rows,
    bound_rows,
    bound_blocks,
    bound_values,
    hub_rows,
    hub_weights,
):
    width = weight.shape[1]
    slot = send_rows.shape[1]
    dom_count, sub_count = lax.axis_size("dom"), lax.axis_size("sub")
    core = (lax.axis_index("dom") % CORES).astype(jnp.int32).reshape(1)
    other_core = [(i, i ^ 1) for i in range(dom_count)]
    same_core = [
        [i for i in range(dom_count * sub_count) if (i // sub_count) % CORES == c] for c in range(CORES)
    ]

    send_own = send_rows.T
    send_other = lax.ppermute(send_own, "dom", other_core)
    near_features = lax.ppermute(features, "dom", other_core)
    mapped, messages = messages_of(core, send_own, send_other, hub_rows, features, near_features, weight)
    arrived = lax.all_to_all(
        messages.reshape(len(same_core[0]), -1, width),
        ("dom", "sub"),
        split_axis=0,
        concat_axis=0,
        tiled=True,
        axis_index_groups=same_core,
    ).reshape(-1, width)
    near = near_part(local_rows, local_blocks, local_values, mapped, layer_bias[None, :])
    received, own_hub = order_rows(core, arrived, slot, near)
    other_hub = lax.ppermute(own_hub, "dom", other_core)
    total = add_far_part(bound_rows, bound_blocks, bound_values, received, near)
    return finish(core, total, hub_weights, own_hub, other_hub)


def solution(mesh):
    in_specs = (
        P(("dom", "sub"), None),
        P(),
        P(),
        P(("dom", "sub")),
        P(("dom", "sub")),
        P(("dom", "sub"), None, None),
        P(("dom", "sub"), None),
        P(("dom", "sub")),
        P(("dom", "sub")),
        P(("dom", "sub"), None, None),
        P(("dom", "sub")),
        P(("dom", "sub"), None),
    )
    out_specs = P(("dom", "sub"), None)
    return jax.shard_map(
        on_device, mesh=mesh, in_specs=in_specs, out_specs=out_specs, check_vma=False
    )
```

```python
import functools

import jax
import jax.numpy as jnp
from jax import lax
from jax.experimental import pallas as pl
from jax.experimental.pallas import tpu as pltpu
from jax.sharding import PartitionSpec as P

VMEM = pl.BlockSpec(memory_space=pltpu.VMEM)
SMEM = pl.BlockSpec(memory_space=pltpu.SMEM)
MIB = 1024 * 1024
Y, Z, CORES, X = 4, 8, 2, 4


PIECES = 4


def send_kernel(
    core_ref, own_hbm, other_hbm, hub_hbm, feat_hbm, near_feat_hbm, weight_hbm, mapped_hbm, message_hbm,
    own, other, hub, feat, near_feat, weight, mapped, table, near_table, stage, out, sems, out_sems
):
    pairs = (
        (feat_hbm, feat), (weight_hbm, weight), (near_feat_hbm, near_feat),
        (own_hbm, own), (other_hbm, other), (hub_hbm, hub),
    )
    copies = [pltpu.make_async_copy(src, dst, sems.at[i]) for i, (src, dst) in enumerate(pairs)]
    for copy in copies:
        copy.start()
    slot = own.shape[0]
    hubs = hub.shape[0]
    message = 2 * slot + hubs
    core = core_ref[0]
    copies[0].wait()
    copies[1].wait()
    mapped_rows = jnp.dot(feat[...], weight[...], preferred_element_type=jnp.float32).astype(jnp.bfloat16)
    mapped[...] = mapped_rows
    table[...] = mapped_rows.astype(jnp.float32)
    sends = [pltpu.make_async_copy(mapped, mapped_hbm, out_sems.at[PIECES])]
    sends[0].start()
    copies[2].wait()
    far = jnp.dot(near_feat[...], weight[...], preferred_element_type=jnp.float32)
    near_table[...] = far.astype(jnp.bfloat16).astype(jnp.float32)
    for copy in copies[3:]:
        copy.wait()
    hub_rows = jnp.concatenate([table[pl.ds(hub[j], 1), :] for j in range(hubs)], axis=0)

    def step(g, carry):
        base = pl.multiple_of(g * (X * message), X * message)
        for x in range(X):
            r = (g * CORES + core) * X + x
            for j in range(slot):
                stage[pl.ds(base + x * message + j, 1), :] = table[pl.ds(own[j, r], 1), :]
            for j in range(slot):
                stage[pl.ds(base + x * message + slot + j, 1), :] = near_table[pl.ds(other[j, r], 1), :]
            stage[pl.ds(base + x * message + 2 * slot, hubs), :] = hub_rows
        return carry

    groups = Y * Z // PIECES
    for piece in range(PIECES):
        lax.fori_loop(piece * groups, (piece + 1) * groups, step, 0, unroll=2)
        rows = pl.ds(piece * groups * X * message, groups * X * message)
        out[rows, :] = stage[rows, :].astype(jnp.bfloat16)
        copy = pltpu.make_async_copy(out.at[rows], message_hbm.at[rows], out_sems.at[piece])
        copy.start()
        sends.append(copy)
    for copy in sends:
        copy.wait()


HBM = pl.BlockSpec(memory_space=pltpu.HBM)


def messages_of(core, send_own, send_other, hub_rows, features, near_features, weight):
    rows, width = features.shape[0], weight.shape[1]
    slot, hubs = send_own.shape[0], hub_rows.shape[0]
    total = Y * Z * X * (2 * slot + hubs)
    return pl.pallas_call(
        send_kernel,
        out_shape=(
            jax.ShapeDtypeStruct((rows, width), jnp.bfloat16),
            jax.ShapeDtypeStruct((total, width), jnp.bfloat16),
        ),
        in_specs=[SMEM, HBM, HBM, HBM, HBM, HBM, HBM],
        out_specs=(HBM, HBM),
        scratch_shapes=[
            pltpu.SMEM(send_own.shape, jnp.int32),
            pltpu.SMEM(send_own.shape, jnp.int32),
            pltpu.SMEM(hub_rows.shape, jnp.int32),
            pltpu.VMEM(features.shape, jnp.bfloat16),
            pltpu.VMEM(features.shape, jnp.bfloat16),
            pltpu.VMEM(weight.shape, jnp.bfloat16),
            pltpu.VMEM((rows, width), jnp.bfloat16),
            pltpu.VMEM((rows, width), jnp.float32),
            pltpu.VMEM((rows, width), jnp.float32),
            pltpu.VMEM((total, width), jnp.float32),
            pltpu.VMEM((total, width), jnp.bfloat16),
            pltpu.SemaphoreType.DMA((6,)),
            pltpu.SemaphoreType.DMA((PIECES + 1,)),
        ],
        compiler_params=pltpu.CompilerParams(vmem_limit_bytes=56 * MIB),
        cost_estimate=pl.CostEstimate(flops=4 * rows * width * width, bytes_accessed=2 * MIB, transcendentals=0),
        name="messages",
    )(core, send_own, send_other, hub_rows, features, near_features, weight)


def near_kernel(rows_ref, blocks_ref, values_ref, mapped_ref, bias_ref, out_ref):
    tile = values_ref.shape[1]
    out_ref[...] = jnp.broadcast_to(bias_ref[...], out_ref.shape)

    def step(t, carry):
        rows = pl.ds(pl.multiple_of(rows_ref[t] * tile, tile), tile)
        block = pl.ds(pl.multiple_of(blocks_ref[t] * tile, tile), tile)
        out_ref[rows, :] += jnp.dot(values_ref[t], mapped_ref[block, :], preferred_element_type=jnp.float32)
        return carry

    lax.fori_loop(0, values_ref.shape[0], step, 0, unroll=32)


def near_part(rows_of, blocks_of, values, mapped, bias):
    tiles, tile = values.shape[:2]
    rows, width = mapped.shape
    return pl.pallas_call(
        near_kernel,
        out_shape=jax.ShapeDtypeStruct((rows, width), jnp.float32),
        in_specs=[SMEM, SMEM, VMEM, VMEM, VMEM],
        out_specs=VMEM,
        compiler_params=pltpu.CompilerParams(vmem_limit_bytes=16 * MIB),
        cost_estimate=pl.CostEstimate(
            flops=2 * tiles * tile * tile * width, bytes_accessed=4 * MIB, transcendentals=0
        ),
        name="near_part",
    )(rows_of, blocks_of, values, mapped, bias)


def order_kernel(slot, core_ref, arrived_ref, after_ref, received_ref, hub_ref):
    message = arrived_ref.shape[0] // (Y * Z * X)
    hubs = message - 2 * slot
    size = X * message
    bound = CORES * X * slot
    core = core_ref[0]
    n = lax.broadcasted_iota(jnp.int32, (size, size), 0)
    source = lax.broadcasted_iota(jnp.int32, (size, size), 1)
    sender = (n >= X * slot).astype(jnp.int32)
    place = n - sender * (X * slot)
    x = sum((place >= k * slot).astype(jnp.int32) for k in range(1, X))
    second = jnp.where(sender == core, 0, slot)
    wanted = x * message + second + (place - x * slot)
    hub_place = n - bound
    hub_x = sum((hub_place >= k * hubs).astype(jnp.int32) for k in range(1, X))
    wanted = jnp.where(n >= bound, hub_x * message + 2 * slot + (hub_place - hub_x * hubs), wanted)
    order = jnp.where(wanted == source, 1.0, 0.0).astype(jnp.bfloat16)

    def step(g, carry):
        chunk = arrived_ref[pl.ds(pl.multiple_of(g * size, size), size), :]
        sorted_rows = jnp.dot(order, chunk, preferred_element_type=jnp.float32).astype(jnp.bfloat16)
        received_ref[pl.ds(pl.multiple_of(g * bound, bound), bound), :] = sorted_rows[:bound]
        hub_ref[pl.ds(pl.multiple_of(g * X * hubs, X * hubs), X * hubs), :] = sorted_rows[bound:]
        return carry

    lax.fori_loop(0, Y * Z, step, 0, unroll=16)


def order_rows(core, arrived, slot, after):
    total, width = arrived.shape
    groups = Y * Z
    bound = groups * CORES * X * slot
    hubs = total - bound
    return pl.pallas_call(
        functools.partial(order_kernel, slot),
        out_shape=(
            jax.ShapeDtypeStruct((bound, width), jnp.bfloat16),
            jax.ShapeDtypeStruct((hubs, width), jnp.bfloat16),
        ),
        in_specs=[SMEM, VMEM, pl.BlockSpec(memory_space=pl.ANY)],
        out_specs=(VMEM, VMEM),
        compiler_params=pltpu.CompilerParams(vmem_limit_bytes=16 * MIB),
        cost_estimate=pl.CostEstimate(flops=8000000000, bytes_accessed=16 * MIB, transcendentals=0),
        name="order_rows",
    )(core, arrived, after)


def far_kernel(rows_ref, blocks_ref, values_ref, received_ref, near_ref, out_ref):
    tile = values_ref.shape[1]
    out_ref[...] = near_ref[...]

    def step(t, carry):
        rows = pl.ds(pl.multiple_of(rows_ref[t] * tile, tile), tile)
        block = pl.ds(pl.multiple_of(blocks_ref[t] * tile, tile), tile)
        out_ref[rows, :] += jnp.dot(values_ref[t], received_ref[block, :], preferred_element_type=jnp.float32)
        return carry

    lax.fori_loop(0, values_ref.shape[0], step, 0, unroll=32)


def add_far_part(rows_of, blocks_of, values, received, near):
    tiles, tile = values.shape[:2]
    rows, width = near.shape
    return pl.pallas_call(
        far_kernel,
        out_shape=jax.ShapeDtypeStruct((rows, width), jnp.float32),
        in_specs=[SMEM, SMEM, VMEM, VMEM, VMEM],
        out_specs=VMEM,
        compiler_params=pltpu.CompilerParams(vmem_limit_bytes=16 * MIB),
        cost_estimate=pl.CostEstimate(
            flops=2 * tiles * tile * tile * width, bytes_accessed=5 * MIB, transcendentals=0
        ),
        name="far_part",
    )(rows_of, blocks_of, values, received, near)


def hub_kernel(core_ref, sum_ref, weights_ref, own_ref, other_ref, out_ref, hub):
    groups = Y * Z
    half = own_ref.shape[0] // groups
    core = core_ref[0]

    def place(g, carry):
        rows = pl.ds(pl.multiple_of(g * half, half), half)
        own_at = pl.multiple_of((g * CORES + core) * half, half)
        other_at = pl.multiple_of((g * CORES + 1 - core) * half, half)
        hub[pl.ds(own_at, half), :] = own_ref[rows, :]
        hub[pl.ds(other_at, half), :] = other_ref[rows, :]
        return carry

    lax.fori_loop(0, groups, place, 0, unroll=8)
    tile = 256

    def step(i, carry):
        rows = pl.ds(pl.multiple_of(i * tile, tile), tile)
        total = sum_ref[rows, :] + jnp.dot(weights_ref[rows, :], hub[...], preferred_element_type=jnp.float32)
        out_ref[rows, :] = jnp.maximum(total, 0.0).astype(out_ref.dtype)
        return carry

    lax.fori_loop(0, out_ref.shape[0] // tile, step, 0, unroll=True)


def finish(core, total, weights, own_hub, other_hub):
    rows, width = total.shape
    hubs = weights.shape[1]
    return pl.pallas_call(
        hub_kernel,
        out_shape=jax.ShapeDtypeStruct((rows, width), jnp.bfloat16),
        in_specs=[SMEM, VMEM, VMEM, VMEM, VMEM],
        out_specs=VMEM,
        scratch_shapes=[pltpu.VMEM((hubs, width), jnp.bfloat16)],
        compiler_params=pltpu.CompilerParams(vmem_limit_bytes=16 * MIB),
        cost_estimate=pl.CostEstimate(flops=2 * rows * hubs * width, bytes_accessed=6 * MIB, transcendentals=0),
        name="hub_part",
    )(core, total, weights, own_hub, other_hub)


def on_device(
    features,
    weight,
    layer_bias,
    local_rows,
    local_blocks,
    local_values,
    send_rows,
    bound_rows,
    bound_blocks,
    bound_values,
    hub_rows,
    hub_weights,
):
    width = weight.shape[1]
    slot = send_rows.shape[1]
    dom_count, sub_count = lax.axis_size("dom"), lax.axis_size("sub")
    core = (lax.axis_index("dom") % CORES).astype(jnp.int32).reshape(1)
    other_core = [(i, i ^ 1) for i in range(dom_count)]
    same_core = [
        [i for i in range(dom_count * sub_count) if (i // sub_count) % CORES == c] for c in range(CORES)
    ]

    send_own = send_rows.T
    send_other = lax.ppermute(send_own, "dom", other_core)
    near_features = lax.ppermute(features, "dom", other_core)
    mapped, messages = messages_of(core, send_own, send_other, hub_rows, features, near_features, weight)
    arrived = lax.all_to_all(
        messages.reshape(len(same_core[0]), -1, width),
        ("dom", "sub"),
        split_axis=0,
        concat_axis=0,
        tiled=True,
        axis_index_groups=same_core,
    ).reshape(-1, width)
    near = near_part(local_rows, local_blocks, local_values, mapped, layer_bias[None, :])
    received, own_hub = order_rows(core, arrived, slot, near)
    other_hub = lax.ppermute(own_hub, "dom", other_core)
    total = add_far_part(bound_rows, bound_blocks, bound_values, received, near)
    return finish(core, total, hub_weights, own_hub, other_hub)


def solution(mesh):
    in_specs = (
        P(("dom", "sub"), None),
        P(),
        P(),
        P(("dom", "sub")),
        P(("dom", "sub")),
        P(("dom", "sub"), None, None),
        P(("dom", "sub"), None),
        P(("dom", "sub")),
        P(("dom", "sub")),
        P(("dom", "sub"), None, None),
        P(("dom", "sub")),
        P(("dom", "sub"), None),
    )
    out_specs = P(("dom", "sub"), None)
    return jax.shard_map(
        on_device, mesh=mesh, in_specs=in_specs, out_specs=out_specs, check_vma=False
    )
```

```python
import functools

import jax
import jax.numpy as jnp
from jax import lax
from jax.experimental import pallas as pl
from jax.experimental.pallas import tpu as pltpu
from jax.sharding import PartitionSpec as P

VMEM = pl.BlockSpec(memory_space=pltpu.VMEM)
SMEM = pl.BlockSpec(memory_space=pltpu.SMEM)
MIB = 1024 * 1024
Y, Z, CORES, X = 4, 8, 2, 4


PIECES = 4


def send_kernel(
    core_ref, own_hbm, other_hbm, hub_hbm, feat_hbm, near_feat_hbm, weight_hbm, mapped_hbm, message_hbm,
    own, other, hub, feat, near_feat, weight, mapped, table, near_table, stage, out, sems, out_sems
):
    pairs = (
        (feat_hbm, feat), (weight_hbm, weight), (near_feat_hbm, near_feat),
        (own_hbm, own), (other_hbm, other), (hub_hbm, hub),
    )
    copies = [pltpu.make_async_copy(src, dst, sems.at[i]) for i, (src, dst) in enumerate(pairs)]
    for copy in copies:
        copy.start()
    slot = own.shape[0]
    hubs = hub.shape[0]
    message = 2 * slot + hubs
    core = core_ref[0]
    copies[0].wait()
    copies[1].wait()
    mapped_rows = jnp.dot(feat[...], weight[...], preferred_element_type=jnp.float32).astype(jnp.bfloat16)
    mapped[...] = mapped_rows
    table[...] = mapped_rows.astype(jnp.float32)
    sends = [pltpu.make_async_copy(mapped, mapped_hbm, out_sems.at[PIECES])]
    sends[0].start()
    copies[2].wait()
    far = jnp.dot(near_feat[...], weight[...], preferred_element_type=jnp.float32)
    near_table[...] = far.astype(jnp.bfloat16).astype(jnp.float32)
    for copy in copies[3:]:
        copy.wait()
    hub_rows = jnp.concatenate([table[pl.ds(hub[j], 1), :] for j in range(hubs)], axis=0)

    def step(g, carry):
        base = pl.multiple_of(g * (X * message), X * message)
        for x in range(X):
            r = (g * CORES + core) * X + x
            for j in range(slot):
                stage[pl.ds(base + x * message + j, 1), :] = table[pl.ds(own[j, r], 1), :]
            for j in range(slot):
                stage[pl.ds(base + x * message + slot + j, 1), :] = near_table[pl.ds(other[j, r], 1), :]
            stage[pl.ds(base + x * message + 2 * slot, hubs), :] = hub_rows
        return carry

    groups = Y * Z // PIECES
    for piece in range(PIECES):
        lax.fori_loop(piece * groups, (piece + 1) * groups, step, 0, unroll=2)
        rows = pl.ds(piece * groups * X * message, groups * X * message)
        out[rows, :] = stage[rows, :].astype(jnp.bfloat16)
        copy = pltpu.make_async_copy(out.at[rows], message_hbm.at[rows], out_sems.at[piece])
        copy.start()
        sends.append(copy)
    for copy in sends:
        copy.wait()


HBM = pl.BlockSpec(memory_space=pltpu.HBM)


def messages_of(core, send_own, send_other, hub_rows, features, near_features, weight):
    rows, width = features.shape[0], weight.shape[1]
    slot, hubs = send_own.shape[0], hub_rows.shape[0]
    total = Y * Z * X * (2 * slot + hubs)
    return pl.pallas_call(
        send_kernel,
        out_shape=(
            jax.ShapeDtypeStruct((rows, width), jnp.bfloat16),
            jax.ShapeDtypeStruct((total, width), jnp.bfloat16),
        ),
        in_specs=[SMEM, HBM, HBM, HBM, HBM, HBM, HBM],
        out_specs=(HBM, HBM),
        scratch_shapes=[
            pltpu.SMEM(send_own.shape, jnp.int32),
            pltpu.SMEM(send_own.shape, jnp.int32),
            pltpu.SMEM(hub_rows.shape, jnp.int32),
            pltpu.VMEM(features.shape, jnp.bfloat16),
            pltpu.VMEM(features.shape, jnp.bfloat16),
            pltpu.VMEM(weight.shape, jnp.bfloat16),
            pltpu.VMEM((rows, width), jnp.bfloat16),
            pltpu.VMEM((rows, width), jnp.float32),
            pltpu.VMEM((rows, width), jnp.float32),
            pltpu.VMEM((total, width), jnp.float32),
            pltpu.VMEM((total, width), jnp.bfloat16),
            pltpu.SemaphoreType.DMA((6,)),
            pltpu.SemaphoreType.DMA((PIECES + 1,)),
        ],
        compiler_params=pltpu.CompilerParams(vmem_limit_bytes=56 * MIB),
        cost_estimate=pl.CostEstimate(flops=4 * rows * width * width, bytes_accessed=2 * MIB, transcendentals=0),
        name="messages",
    )(core, send_own, send_other, hub_rows, features, near_features, weight)


def near_kernel(rows_ref, blocks_ref, values_ref, mapped_ref, bias_ref, out_ref):
    tile = values_ref.shape[1]
    out_ref[...] = jnp.broadcast_to(bias_ref[...], out_ref.shape)

    def step(t, carry):
        rows = pl.ds(pl.multiple_of(rows_ref[t] * tile, tile), tile)
        block = pl.ds(pl.multiple_of(blocks_ref[t] * tile, tile), tile)
        out_ref[rows, :] += jnp.dot(values_ref[t], mapped_ref[block, :], preferred_element_type=jnp.float32)
        return carry

    lax.fori_loop(0, values_ref.shape[0], step, 0, unroll=32)


def near_part(rows_of, blocks_of, values, mapped, bias):
    tiles, tile = values.shape[:2]
    rows, width = mapped.shape
    return pl.pallas_call(
        near_kernel,
        out_shape=jax.ShapeDtypeStruct((rows, width), jnp.float32),
        in_specs=[SMEM, SMEM, VMEM, VMEM, VMEM],
        out_specs=VMEM,
        compiler_params=pltpu.CompilerParams(vmem_limit_bytes=16 * MIB),
        cost_estimate=pl.CostEstimate(
            flops=2 * tiles * tile * tile * width, bytes_accessed=4 * MIB, transcendentals=0
        ),
        name="near_part",
    )(rows_of, blocks_of, values, mapped, bias)


def order_kernel(slot, core_ref, arrived_ref, received_ref, hub_ref):
    message = arrived_ref.shape[0] // (Y * Z * X)
    hubs = message - 2 * slot
    size = X * message
    bound = CORES * X * slot
    core = core_ref[0]
    n = lax.broadcasted_iota(jnp.int32, (size, size), 0)
    source = lax.broadcasted_iota(jnp.int32, (size, size), 1)
    sender = (n >= X * slot).astype(jnp.int32)
    place = n - sender * (X * slot)
    x = sum((place >= k * slot).astype(jnp.int32) for k in range(1, X))
    second = jnp.where(sender == core, 0, slot)
    wanted = x * message + second + (place - x * slot)
    hub_place = n - bound
    hub_x = sum((hub_place >= k * hubs).astype(jnp.int32) for k in range(1, X))
    wanted = jnp.where(n >= bound, hub_x * message + 2 * slot + (hub_place - hub_x * hubs), wanted)
    order = jnp.where(wanted == source, 1.0, 0.0).astype(jnp.bfloat16)

    def step(g, carry):
        chunk = arrived_ref[pl.ds(pl.multiple_of(g * size, size), size), :]
        sorted_rows = jnp.dot(order, chunk, preferred_element_type=jnp.float32).astype(jnp.bfloat16)
        received_ref[pl.ds(pl.multiple_of(g * bound, bound), bound), :] = sorted_rows[:bound]
        hub_ref[pl.ds(pl.multiple_of(g * X * hubs, X * hubs), X * hubs), :] = sorted_rows[bound:]
        return carry

    lax.fori_loop(0, Y * Z, step, 0, unroll=32)


def order_rows(core, arrived, slot):
    total, width = arrived.shape
    groups = Y * Z
    bound = groups * CORES * X * slot
    hubs = total - bound
    return pl.pallas_call(
        functools.partial(order_kernel, slot),
        out_shape=(
            jax.ShapeDtypeStruct((bound, width), jnp.bfloat16),
            jax.ShapeDtypeStruct((hubs, width), jnp.bfloat16),
        ),
        in_specs=[SMEM, VMEM],
        out_specs=(VMEM, VMEM),
        compiler_params=pltpu.CompilerParams(vmem_limit_bytes=16 * MIB),
        cost_estimate=pl.CostEstimate(flops=8000000000, bytes_accessed=16 * MIB, transcendentals=0),
        name="order_rows",
    )(core, arrived)


def far_kernel(rows_ref, blocks_ref, values_ref, received_ref, near_ref, out_ref):
    tile = values_ref.shape[1]
    out_ref[...] = near_ref[...]

    def step(t, carry):
        rows = pl.ds(pl.multiple_of(rows_ref[t] * tile, tile), tile)
        block = pl.ds(pl.multiple_of(blocks_ref[t] * tile, tile), tile)
        out_ref[rows, :] += jnp.dot(values_ref[t], received_ref[block, :], preferred_element_type=jnp.float32)
        return carry

    lax.fori_loop(0, values_ref.shape[0], step, 0, unroll=96)


def add_far_part(rows_of, blocks_of, values, received, near):
    tiles, tile = values.shape[:2]
    rows, width = near.shape
    return pl.pallas_call(
        far_kernel,
        out_shape=jax.ShapeDtypeStruct((rows, width), jnp.float32),
        in_specs=[SMEM, SMEM, VMEM, VMEM, VMEM],
        out_specs=VMEM,
        compiler_params=pltpu.CompilerParams(vmem_limit_bytes=16 * MIB),
        cost_estimate=pl.CostEstimate(
            flops=2 * tiles * tile * tile * width, bytes_accessed=5 * MIB, transcendentals=0
        ),
        name="far_part",
    )(rows_of, blocks_of, values, received, near)


def hub_kernel(core_ref, sum_ref, weights_ref, own_ref, other_ref, out_ref, hub):
    groups = Y * Z
    half = own_ref.shape[0] // groups
    core = core_ref[0]

    def place(g, carry):
        rows = pl.ds(pl.multiple_of(g * half, half), half)
        own_at = pl.multiple_of((g * CORES + core) * half, half)
        other_at = pl.multiple_of((g * CORES + 1 - core) * half, half)
        hub[pl.ds(own_at, half), :] = own_ref[rows, :]
        hub[pl.ds(other_at, half), :] = other_ref[rows, :]
        return carry

    lax.fori_loop(0, groups, place, 0, unroll=16)
    tile = 256

    def step(i, carry):
        rows = pl.ds(pl.multiple_of(i * tile, tile), tile)
        total = sum_ref[rows, :] + jnp.dot(weights_ref[rows, :], hub[...], preferred_element_type=jnp.float32)
        out_ref[rows, :] = jnp.maximum(total, 0.0).astype(out_ref.dtype)
        return carry

    lax.fori_loop(0, out_ref.shape[0] // tile, step, 0, unroll=True)


def finish(core, total, weights, own_hub, other_hub):
    rows, width = total.shape
    hubs = weights.shape[1]
    return pl.pallas_call(
        hub_kernel,
        out_shape=jax.ShapeDtypeStruct((rows, width), jnp.bfloat16),
        in_specs=[SMEM, VMEM, VMEM, VMEM, VMEM],
        out_specs=VMEM,
        scratch_shapes=[pltpu.VMEM((hubs, width), jnp.bfloat16)],
        compiler_params=pltpu.CompilerParams(vmem_limit_bytes=16 * MIB),
        cost_estimate=pl.CostEstimate(flops=2 * rows * hubs * width, bytes_accessed=6 * MIB, transcendentals=0),
        name="hub_part",
    )(core, total, weights, own_hub, other_hub)


def on_device(
    features,
    weight,
    layer_bias,
    local_rows,
    local_blocks,
    local_values,
    send_rows,
    bound_rows,
    bound_blocks,
    bound_values,
    hub_rows,
    hub_weights,
):
    width = weight.shape[1]
    slot = send_rows.shape[1]
    dom_count, sub_count = lax.axis_size("dom"), lax.axis_size("sub")
    core = (lax.axis_index("dom") % CORES).astype(jnp.int32).reshape(1)
    other_core = [(i, i ^ 1) for i in range(dom_count)]
    same_core = [
        [i for i in range(dom_count * sub_count) if (i // sub_count) % CORES == c] for c in range(CORES)
    ]

    send_own = send_rows.T
    send_other = lax.ppermute(send_own, "dom", other_core)
    near_features = lax.ppermute(features, "dom", other_core)
    mapped, messages = messages_of(core, send_own, send_other, hub_rows, features, near_features, weight)
    arrived = lax.all_to_all(
        messages.reshape(len(same_core[0]), -1, width),
        ("dom", "sub"),
        split_axis=0,
        concat_axis=0,
        tiled=True,
        axis_index_groups=same_core,
    ).reshape(-1, width)
    near = near_part(local_rows, local_blocks, local_values, mapped, layer_bias[None, :])
    arrived, near = lax.optimization_barrier((arrived, near))
    received, own_hub = order_rows(core, arrived, slot)
    other_hub = lax.ppermute(own_hub, "dom", other_core)
    total = add_far_part(bound_rows, bound_blocks, bound_values, received, near)
    return finish(core, total, hub_weights, own_hub, other_hub)


def solution(mesh):
    in_specs = (
        P(("dom", "sub"), None),
        P(),
        P(),
        P(("dom", "sub")),
        P(("dom", "sub")),
        P(("dom", "sub"), None, None),
        P(("dom", "sub"), None),
        P(("dom", "sub")),
        P(("dom", "sub")),
        P(("dom", "sub"), None, None),
        P(("dom", "sub")),
        P(("dom", "sub"), None),
    )
    out_specs = P(("dom", "sub"), None)
    return jax.shard_map(
        on_device, mesh=mesh, in_specs=in_specs, out_specs=out_specs, check_vma=False
    )
```

```python
import functools

import jax
import jax.numpy as jnp
from jax import lax
from jax.experimental import pallas as pl
from jax.experimental.pallas import tpu as pltpu
from jax.sharding import PartitionSpec as P

VMEM = pl.BlockSpec(memory_space=pltpu.VMEM)
SMEM = pl.BlockSpec(memory_space=pltpu.SMEM)
MIB = 1024 * 1024
Y, Z, CORES, X = 4, 8, 2, 4


PIECES = 4


def send_kernel(
    core_ref, own_hbm, other_hbm, hub_hbm, feat_hbm, near_feat_hbm, weight_hbm, mapped_hbm, message_hbm,
    own, other, hub, feat, near_feat, weight, mapped, table, near_table, stage, out, sems, out_sems
):
    pairs = (
        (feat_hbm, feat), (weight_hbm, weight), (near_feat_hbm, near_feat),
        (own_hbm, own), (other_hbm, other), (hub_hbm, hub),
    )
    copies = [pltpu.make_async_copy(src, dst, sems.at[i]) for i, (src, dst) in enumerate(pairs)]
    for copy in copies:
        copy.start()
    slot = own.shape[0]
    hubs = hub.shape[0]
    message = 2 * slot + hubs
    core = core_ref[0]
    copies[0].wait()
    copies[1].wait()
    mapped_rows = jnp.dot(feat[...], weight[...], preferred_element_type=jnp.float32).astype(jnp.bfloat16)
    mapped[...] = mapped_rows
    table[...] = mapped_rows.astype(jnp.float32)
    sends = [pltpu.make_async_copy(mapped, mapped_hbm, out_sems.at[PIECES])]
    sends[0].start()
    copies[2].wait()
    far = jnp.dot(near_feat[...], weight[...], preferred_element_type=jnp.float32)
    near_table[...] = far.astype(jnp.bfloat16).astype(jnp.float32)
    for copy in copies[3:]:
        copy.wait()
    hub_rows = jnp.concatenate([table[pl.ds(hub[j], 1), :] for j in range(hubs)], axis=0)

    def step(g, carry):
        base = pl.multiple_of(g * (X * message), X * message)
        for x in range(X):
            r = (g * CORES + core) * X + x
            for j in range(slot):
                stage[pl.ds(base + x * message + j, 1), :] = table[pl.ds(own[j, r], 1), :]
            for j in range(slot):
                stage[pl.ds(base + x * message + slot + j, 1), :] = near_table[pl.ds(other[j, r], 1), :]
            stage[pl.ds(base + x * message + 2 * slot, hubs), :] = hub_rows
        return carry

    groups = Y * Z // PIECES
    for piece in range(PIECES):
        lax.fori_loop(piece * groups, (piece + 1) * groups, step, 0, unroll=8)
        rows = pl.ds(piece * groups * X * message, groups * X * message)
        out[rows, :] = stage[rows, :].astype(jnp.bfloat16)
        copy = pltpu.make_async_copy(out.at[rows], message_hbm.at[rows], out_sems.at[piece])
        copy.start()
        sends.append(copy)
    for copy in sends:
        copy.wait()


HBM = pl.BlockSpec(memory_space=pltpu.HBM)


def messages_of(core, send_own, send_other, hub_rows, features, near_features, weight):
    rows, width = features.shape[0], weight.shape[1]
    slot, hubs = send_own.shape[0], hub_rows.shape[0]
    total = Y * Z * X * (2 * slot + hubs)
    return pl.pallas_call(
        send_kernel,
        out_shape=(
            jax.ShapeDtypeStruct((rows, width), jnp.bfloat16),
            jax.ShapeDtypeStruct((total, width), jnp.bfloat16),
        ),
        in_specs=[SMEM, HBM, HBM, HBM, HBM, HBM, HBM],
        out_specs=(HBM, HBM),
        scratch_shapes=[
            pltpu.SMEM(send_own.shape, jnp.int32),
            pltpu.SMEM(send_own.shape, jnp.int32),
            pltpu.SMEM(hub_rows.shape, jnp.int32),
            pltpu.VMEM(features.shape, jnp.bfloat16),
            pltpu.VMEM(features.shape, jnp.bfloat16),
            pltpu.VMEM(weight.shape, jnp.bfloat16),
            pltpu.VMEM((rows, width), jnp.bfloat16),
            pltpu.VMEM((rows, width), jnp.float32),
            pltpu.VMEM((rows, width), jnp.float32),
            pltpu.VMEM((total, width), jnp.float32),
            pltpu.VMEM((total, width), jnp.bfloat16),
            pltpu.SemaphoreType.DMA((6,)),
            pltpu.SemaphoreType.DMA((PIECES + 1,)),
        ],
        compiler_params=pltpu.CompilerParams(vmem_limit_bytes=56 * MIB),
        cost_estimate=pl.CostEstimate(flops=4 * rows * width * width, bytes_accessed=2 * MIB, transcendentals=0),
        name="messages",
    )(core, send_own, send_other, hub_rows, features, near_features, weight)


def near_kernel(rows_ref, blocks_ref, values_ref, mapped_ref, bias_ref, out_ref):
    tile = values_ref.shape[1]
    out_ref[...] = jnp.broadcast_to(bias_ref[...], out_ref.shape)

    def step(t, carry):
        rows = pl.ds(pl.multiple_of(rows_ref[t] * tile, tile), tile)
        block = pl.ds(pl.multiple_of(blocks_ref[t] * tile, tile), tile)
        out_ref[rows, :] += jnp.dot(values_ref[t], mapped_ref[block, :], preferred_element_type=jnp.float32)
        return carry

    lax.fori_loop(0, values_ref.shape[0], step, 0, unroll=32)


def near_part(rows_of, blocks_of, values, mapped, bias):
    tiles, tile = values.shape[:2]
    rows, width = mapped.shape
    return pl.pallas_call(
        near_kernel,
        out_shape=jax.ShapeDtypeStruct((rows, width), jnp.float32),
        in_specs=[SMEM, SMEM, VMEM, VMEM, VMEM],
        out_specs=VMEM,
        compiler_params=pltpu.CompilerParams(vmem_limit_bytes=16 * MIB),
        cost_estimate=pl.CostEstimate(
            flops=2 * tiles * tile * tile * width, bytes_accessed=4 * MIB, transcendentals=0
        ),
        name="near_part",
    )(rows_of, blocks_of, values, mapped, bias)


def order_kernel(slot, core_ref, arrived_ref, received_ref, hub_ref):
    message = arrived_ref.shape[0] // (Y * Z * X)
    hubs = message - 2 * slot
    size = X * message
    bound = CORES * X * slot
    core = core_ref[0]
    n = lax.broadcasted_iota(jnp.int32, (size, size), 0)
    source = lax.broadcasted_iota(jnp.int32, (size, size), 1)
    sender = (n >= X * slot).astype(jnp.int32)
    place = n - sender * (X * slot)
    x = sum((place >= k * slot).astype(jnp.int32) for k in range(1, X))
    second = jnp.where(sender == core, 0, slot)
    wanted = x * message + second + (place - x * slot)
    hub_place = n - bound
    hub_x = sum((hub_place >= k * hubs).astype(jnp.int32) for k in range(1, X))
    wanted = jnp.where(n >= bound, hub_x * message + 2 * slot + (hub_place - hub_x * hubs), wanted)
    order = jnp.where(wanted == source, 1.0, 0.0).astype(jnp.bfloat16)

    def step(g, carry):
        chunk = arrived_ref[pl.ds(pl.multiple_of(g * size, size), size), :]
        sorted_rows = jnp.dot(order, chunk, preferred_element_type=jnp.float32).astype(jnp.bfloat16)
        received_ref[pl.ds(pl.multiple_of(g * bound, bound), bound), :] = sorted_rows[:bound]
        hub_ref[pl.ds(pl.multiple_of(g * X * hubs, X * hubs), X * hubs), :] = sorted_rows[bound:]
        return carry

    lax.fori_loop(0, Y * Z, step, 0, unroll=32)


def order_rows(core, arrived, slot):
    total, width = arrived.shape
    groups = Y * Z
    bound = groups * CORES * X * slot
    hubs = total - bound
    return pl.pallas_call(
        functools.partial(order_kernel, slot),
        out_shape=(
            jax.ShapeDtypeStruct((bound, width), jnp.bfloat16),
            jax.ShapeDtypeStruct((hubs, width), jnp.bfloat16),
        ),
        in_specs=[SMEM, VMEM],
        out_specs=(VMEM, VMEM),
        compiler_params=pltpu.CompilerParams(vmem_limit_bytes=16 * MIB),
        cost_estimate=pl.CostEstimate(flops=8000000000, bytes_accessed=16 * MIB, transcendentals=0),
        name="order_rows",
    )(core, arrived)


def far_kernel(rows_ref, blocks_ref, values_ref, received_ref, near_ref, out_ref):
    tile = values_ref.shape[1]
    out_ref[...] = near_ref[...]

    def step(t, carry):
        rows = pl.ds(pl.multiple_of(rows_ref[t] * tile, tile), tile)
        block = pl.ds(pl.multiple_of(blocks_ref[t] * tile, tile), tile)
        out_ref[rows, :] += jnp.dot(values_ref[t], received_ref[block, :], preferred_element_type=jnp.float32)
        return carry

    lax.fori_loop(0, values_ref.shape[0], step, 0, unroll=96)


def add_far_part(rows_of, blocks_of, values, received, near):
    tiles, tile = values.shape[:2]
    rows, width = near.shape
    return pl.pallas_call(
        far_kernel,
        out_shape=jax.ShapeDtypeStruct((rows, width), jnp.float32),
        in_specs=[SMEM, SMEM, VMEM, VMEM, VMEM],
        out_specs=VMEM,
        compiler_params=pltpu.CompilerParams(vmem_limit_bytes=16 * MIB),
        cost_estimate=pl.CostEstimate(
            flops=2 * tiles * tile * tile * width, bytes_accessed=5 * MIB, transcendentals=0
        ),
        name="far_part",
    )(rows_of, blocks_of, values, received, near)


def hub_kernel(core_ref, sum_ref, weights_ref, own_ref, other_ref, out_ref, hub):
    groups = Y * Z
    half = own_ref.shape[0] // groups
    core = core_ref[0]

    def place(g, carry):
        rows = pl.ds(pl.multiple_of(g * half, half), half)
        own_at = pl.multiple_of((g * CORES + core) * half, half)
        other_at = pl.multiple_of((g * CORES + 1 - core) * half, half)
        hub[pl.ds(own_at, half), :] = own_ref[rows, :]
        hub[pl.ds(other_at, half), :] = other_ref[rows, :]
        return carry

    lax.fori_loop(0, groups, place, 0, unroll=16)
    tile = 256

    def step(i, carry):
        rows = pl.ds(pl.multiple_of(i * tile, tile), tile)
        total = sum_ref[rows, :] + jnp.dot(weights_ref[rows, :], hub[...], preferred_element_type=jnp.float32)
        out_ref[rows, :] = jnp.maximum(total, 0.0).astype(out_ref.dtype)
        return carry

    lax.fori_loop(0, out_ref.shape[0] // tile, step, 0, unroll=True)


def finish(core, total, weights, own_hub, other_hub):
    rows, width = total.shape
    hubs = weights.shape[1]
    return pl.pallas_call(
        hub_kernel,
        out_shape=jax.ShapeDtypeStruct((rows, width), jnp.bfloat16),
        in_specs=[SMEM, VMEM, VMEM, VMEM, VMEM],
        out_specs=VMEM,
        scratch_shapes=[pltpu.VMEM((hubs, width), jnp.bfloat16)],
        compiler_params=pltpu.CompilerParams(vmem_limit_bytes=16 * MIB),
        cost_estimate=pl.CostEstimate(flops=2 * rows * hubs * width, bytes_accessed=6 * MIB, transcendentals=0),
        name="hub_part",
    )(core, total, weights, own_hub, other_hub)


def on_device(
    features,
    weight,
    layer_bias,
    local_rows,
    local_blocks,
    local_values,
    send_rows,
    bound_rows,
    bound_blocks,
    bound_values,
    hub_rows,
    hub_weights,
):
    width = weight.shape[1]
    slot = send_rows.shape[1]
    dom_count, sub_count = lax.axis_size("dom"), lax.axis_size("sub")
    core = (lax.axis_index("dom") % CORES).astype(jnp.int32).reshape(1)
    other_core = [(i, i ^ 1) for i in range(dom_count)]
    same_core = [
        [i for i in range(dom_count * sub_count) if (i // sub_count) % CORES == c] for c in range(CORES)
    ]

    send_own = send_rows.T
    send_other = lax.ppermute(send_own, "dom", other_core)
    near_features = lax.ppermute(features, "dom", other_core)
    mapped, messages = messages_of(core, send_own, send_other, hub_rows, features, near_features, weight)
    arrived = lax.all_to_all(
        messages.reshape(len(same_core[0]), -1, width),
        ("dom", "sub"),
        split_axis=0,
        concat_axis=0,
        tiled=True,
        axis_index_groups=same_core,
    ).reshape(-1, width)
    near = near_part(local_rows, local_blocks, local_values, mapped, layer_bias[None, :])
    arrived, near = lax.optimization_barrier((arrived, near))
    received, own_hub = order_rows(core, arrived, slot)
    other_hub = lax.ppermute(own_hub, "dom", other_core)
    total = add_far_part(bound_rows, bound_blocks, bound_values, received, near)
    return finish(core, total, hub_weights, own_hub, other_hub)


def solution(mesh):
    in_specs = (
        P(("dom", "sub"), None),
        P(),
        P(),
        P(("dom", "sub")),
        P(("dom", "sub")),
        P(("dom", "sub"), None, None),
        P(("dom", "sub"), None),
        P(("dom", "sub")),
        P(("dom", "sub")),
        P(("dom", "sub"), None, None),
        P(("dom", "sub")),
        P(("dom", "sub"), None),
    )
    out_specs = P(("dom", "sub"), None)
    return jax.shard_map(
        on_device, mesh=mesh, in_specs=in_specs, out_specs=out_specs, check_vma=False
    )
```
